32 devices in a mesh: row: 16 (over z, y, core), col: 2 (over x).
Axes of the slice: x: 2, y: 2, z: 4, core: 2. Of those that a mesh axis runs over, the one named last changes fastest.
Arguments:
- tail_factor: bfloat16 [2, 16384, 768], P(None, 'row', 'col'), may hold values from -0.03125 to 0.03125
- tail_solution: bfloat16 [2, 16384, 512], P(None, 'row', 'col'), may hold values from -6 to 6
- coupling: bfloat16 [3, 2, 256, 768], P(None, None, 'row'), may hold values from -0.25 to 0.25
- inverse_blocks: float32 [3, 2, 256, 256], P(None, None, 'row'), may hold values from -0.25 to 1.25
- sources: float32 [3, 2, 256, 512], P(None, None, 'row'), may hold values from -6 to 6
- station_map: int32 [512], P('col'), may hold values from 0 to 511
Outputs:
- solution: float32 [3, 2, 256, 512], P(None, None, 'row', 'col')
The draws below stay inside these ranges and needn't reach their ends.
All inputs are finite; a program needn't handle non-finite values.
Results may differ from the reference program's by a relative error of at most 0.0027.
Values may be sent and summed in bfloat16 or wider, within the bound.
A program may use at most 64 MiB of HBM per device.

```python
import math
import jax
import jax.numpy as jnp
from jax import lax

PW = 256
NP = 3
NSRC = 512
MT = 16384
R = 512
NF = 768


def draw_inverse_blocks(key, part):
    first_key = jax.random.fold_in(key, 17)
    noise = jax.random.normal(first_key, (NP, 2, PW, PW), jnp.float32) * (0.4 / math.sqrt(PW))
    identity = jnp.eye(PW, dtype=jnp.float32)
    diagonal = jnp.stack([identity, jnp.zeros_like(identity)])
    return diagonal[None] + noise


def touch_ends(array, key, low, high):
    place = [jax.random.randint(jax.random.fold_in(key, axis), (), 0, length) for axis, length in enumerate(array.shape)]
    widest = array.shape.index(max(array.shape))
    neighbour = place[:widest] + [(place[widest] + 1) % array.shape[widest]] + place[widest + 1:]
    return array.at[tuple(place)].set(low).at[tuple(neighbour)].set(high)


def shard_levels(stream_key, shape, split, least, largest):
    def one(position, blocks):
        steps = jax.random.uniform(jax.random.fold_in(jax.random.fold_in(stream_key, 6), position), (blocks,), jnp.float32, least / len(split), largest / len(split))
        return jnp.repeat(jnp.exp(steps), shape[position] // blocks).reshape((-1,) + (1,) * (len(shape) - position - 1))

    level = one(*split[0])
    for cut in split[1:]:
        level = level * one(*cut)
    return level


def normal_values(key, shape, scale, bound, split=(), kind=jnp.bfloat16):
    result = scale * jax.random.normal(key, shape, jnp.float32)
    if split:
        result = result * shard_levels(key, shape, split, -0.22, 0.18)
    return jnp.clip(result, -bound, bound).astype(kind)


def setup_inputs(seed: int = 0) -> dict:
    keys = jax.random.split(jax.random.key(seed), 7)
    return {
        "tail_factor": normal_values(keys[0], (2, MT, NF), (2 * MT) ** -0.5, 0.03125, ((1, 16), (2, 2))),
        "tail_solution": normal_values(keys[1], (2, MT, R), 1.0, 6.0, ((1, 16), (2, 2))),
        "coupling": normal_values(keys[2], (NP, 2, PW, NF), (2 * PW) ** -0.5, 0.25, ((2, 16),)),
        "inverse_blocks": draw_inverse_blocks(jax.random.fold_in(keys[6], 71), 0),
        "sources": normal_values(keys[4], (NP, 2, PW, NSRC), 1.0, 6.0, ((2, 16),), jnp.float32),
        "station_map": touch_ends(jax.random.randint(keys[5], (R,), 0, NSRC), jax.random.fold_in(keys[5], 1), 0, NSRC - 1).astype(jnp.int32),
    }


def conj_tproduct(factor_part, solution_part):
    real_part = jnp.dot(factor_part[0].T, solution_part[0], preferred_element_type=jnp.float32) + jnp.dot(factor_part[1].T, solution_part[1], preferred_element_type=jnp.float32)
    imag_part = jnp.dot(factor_part[0].T, solution_part[1], preferred_element_type=jnp.float32) - jnp.dot(factor_part[1].T, solution_part[0], preferred_element_type=jnp.float32)
    return jnp.stack([real_part, imag_part])


def complex_product(matrix, vectors):
    high = lax.Precision.HIGHEST
    real_part = jnp.dot(matrix[0], vectors[0], precision=high) - jnp.dot(matrix[1], vectors[1], precision=high)
    imag_part = jnp.dot(matrix[0], vectors[1], precision=high) + jnp.dot(matrix[1], vectors[0], precision=high)
    return jnp.stack([real_part, imag_part])


def reference(tail_factor, tail_solution, coupling, inverse_blocks, sources, station_map):
    adjoint_rhs = jnp.take(sources, station_map, axis=3)
    partial_value = conj_tproduct(tail_factor, tail_solution).reshape(2, NP, PW, -1)
    solved = [None] * NP
    rounded = [None] * NP
    for panel_index in range(NP - 1, -1, -1):
        pending = partial_value[:, panel_index]
        for later_panel in range(panel_index + 1, NP):
            block_cols = coupling[later_panel][:, :, panel_index * PW:(panel_index + 1) * PW]
            pending = pending + conj_tproduct(block_cols, rounded[later_panel])
        residue = adjoint_rhs[panel_index] - pending
        solved[panel_index] = complex_product(inverse_blocks[panel_index], residue)
        rounded[panel_index] = solved[panel_index].astype(jnp.bfloat16)
    return jnp.stack(solved)
```

```python
import functools

import jax
import jax.numpy as jnp
from jax import lax
from jax.experimental import pallas as pl
from jax.experimental.pallas import tpu as pltpu
from jax.sharding import PartitionSpec as P

MESH = pl.DeviceIdType.MESH


def conj_tproduct(factor_part, solution_part):
    real_part = jnp.einsum(
        "pq,pr->qr", factor_part[0], solution_part[0], preferred_element_type=jnp.float32
    ) + jnp.einsum(
        "pq,pr->qr", factor_part[1], solution_part[1], preferred_element_type=jnp.float32
    )
    imag_part = jnp.einsum(
        "pq,pr->qr", factor_part[0], solution_part[1], preferred_element_type=jnp.float32
    ) - jnp.einsum(
        "pq,pr->qr", factor_part[1], solution_part[0], preferred_element_type=jnp.float32
    )
    return jnp.stack([real_part, imag_part])


def complex_product(matrix, vectors):
    high = lax.Precision.HIGHEST
    real_part = jnp.dot(matrix[0], vectors[0], precision=high) - jnp.dot(
        matrix[1], vectors[1], precision=high
    )
    imag_part = jnp.dot(matrix[0], vectors[1], precision=high) + jnp.dot(
        matrix[1], vectors[0], precision=high
    )
    return jnp.stack([real_part, imag_part])


def shards(tail_factor, tail_solution, coupling, inverse_blocks, sources, station_map):
    panel_count = coupling.shape[0]
    panel_width = inverse_blocks.shape[3]
    local_rows = inverse_blocks.shape[2]
    rhs_local = tail_solution.shape[2]
    source_count = sources.shape[3]
    selector = (
        lax.broadcasted_iota(jnp.int32, (source_count, rhs_local), 0) == station_map[None, :]
    ).astype(jnp.float32)
    adjoint_rhs = jnp.einsum("kcps,sr->kcpr", sources, selector, precision=lax.Precision.HIGHEST)
    partial_value = conj_tproduct(
        lax.all_gather(tail_factor, "col", axis=2, tiled=True), tail_solution
    )
    partial_value = partial_value.reshape(2, panel_count, panel_width, rhs_local)
    solved = [None] * panel_count
    rounded = [None] * panel_count
    row_offset = lax.axis_index("row") * local_rows
    own_rhs = jnp.transpose(adjoint_rhs, (1, 0, 2, 3))
    placed_all = lax.dynamic_update_slice_in_dim(
        jnp.zeros_like(partial_value), own_rhs, row_offset, 2
    )
    base_rhs = lax.psum(placed_all - partial_value, "row")
    whole_coupling = lax.all_gather(coupling, "row", axis=2, tiled=True)
    gathered = [None] * panel_count
    for panel_index in range(panel_count - 1, -1, -1):
        full_y = base_rhs[:, panel_index]
        for later_panel in range(panel_index + 1, panel_count):
            block_cols = whole_coupling[later_panel][
                :, :, panel_index * panel_width : (panel_index + 1) * panel_width
            ]
            full_y = full_y - conj_tproduct(block_cols, gathered[later_panel])
        solved[panel_index] = complex_product(inverse_blocks[panel_index], full_y)
        rounded[panel_index] = solved[panel_index].astype(jnp.bfloat16)
        if panel_index > 0:
            gathered[panel_index] = lax.all_gather(rounded[panel_index], "row", axis=1, tiled=True)
    return jnp.stack(solved)


def split_two(value):
    high = value.astype(jnp.bfloat16)
    low = (value - high.astype(jnp.float32)).astype(jnp.bfloat16)
    return high, low


def dot_tn(left, right):
    return lax.dot_general(
        left, right, (((0,), (0,)), ((), ())), preferred_element_type=jnp.float32
    )


def dot_nt(left, right):
    return lax.dot_general(
        left, right, (((1,), (1,)), ((), ())), preferred_element_type=jnp.float32
    )


def dot_nn(left, right):
    return lax.dot_general(
        left, right, (((1,), (0,)), ((), ())), preferred_element_type=jnp.float32
    )


def panel_pairs(panels):
    return [(j, k) for j in range(panels) for k in range(j)]


def fused_kernel(
    rows, depth, panels, chunks,
    factor, tail, coupling, inverse, sources, station, out,
    rx, part, core_in, core_sum, y_in, y_sum, z_in, reduced, x_in,
    blocks, adj_out, adj_in, sol_out, xs, adj_s, sol_s, core_s, y_s, z_s, swap_s,
    bz_s, by_s, bc_s,
):
    row = lax.axis_index("row")
    col = lax.axis_index("col")
    core = lax.rem(row, 2)
    yy = lax.rem(row // 2, 2)
    zz = row // 4
    width = factor.shape[2]
    local = inverse.shape[2]
    panel = inverse.shape[3]
    span = rows * 8
    lanes = adj_in.shape[3]
    kinds = panels * 2

    def slot_of(r):
        return (lax.rem(r, 2) * 2 + lax.rem(r // 2, 2)) * depth + r // 4

    def row_of(z, y, c):
        return z * 4 + y * 2 + c

    my_slot = slot_of(row)
    peers = [lax.rem(row + d, rows) for d in range(1, rows)]
    core_peer = row_of(zz, yy, 1 - core)
    y_peer = row_of(zz, 1 - yy, core)
    z_hops = [lax.rem(zz + d, depth) for d in range(1, depth)]
    z_from = [lax.rem(zz + depth - d, depth) for d in range(1, depth)]
    pending = []

    def send(source, target, sems, device_row, device_col, *index):
        copy = pltpu.make_async_remote_copy(
            src_ref=source, dst_ref=target,
            send_sem=sems.at[(0, *index)], recv_sem=sems.at[(1, *index)],
            device_id=(device_row, device_col), device_id_type=MESH,
        )
        copy.start()
        pending.append(copy)
        return copy

    barrier = pltpu.get_barrier_semaphore()
    for peer in peers:
        pl.semaphore_signal(barrier, inc=1, device_id=(peer, col), device_id_type=MESH)
    pl.semaphore_signal(barrier, inc=1, device_id=(row, 1 - col), device_id_type=MESH)
    pl.semaphore_wait(barrier, rows)

    x_copies = [
        send(tail.at[:, :, pl.ds(q * span, span)], rx.at[q], xs, row, 1 - col, q)
        for q in range(chunks)
    ]

    pairs = panel_pairs(panels)
    for k in range(panels):
        for c in range(2):
            high, low = split_two(inverse[k, c])
            blocks[row, k * 2 + c] = high
            blocks[row, kinds + k * 2 + c] = low
    for place, (j, k) in enumerate(pairs):
        for c in range(2):
            blocks[row, 2 * kinds + place * 2 + c] = coupling[
                j, c, :, k * panel:(k + 1) * panel
            ]
    bz = [
        send(blocks.at[row], blocks.at[row], bz_s, row_of(z, yy, core), col, d)
        for d, z in enumerate(z_hops)
    ]
    by = [send(blocks.at[row], blocks.at[row], by_s, y_peer, col, 0)]
    bc = [send(blocks.at[row], blocks.at[row], bc_s, core_peer, col, 0)]

    def multiply(real, imag):
        re = dot_tn(real, factor[0]) + dot_tn(imag, factor[1])
        im = dot_tn(imag, factor[0]) - dot_tn(real, factor[1])
        return re, im

    core_copies, y_copies, z_copies = {}, {}, {}

    def stage_core(chunk, real, imag):
        re, im = multiply(real, imag)
        shape = (2, 2, depth, 8, width)
        part[chunk, :, :, :, :, 0:width] = re.reshape(shape)
        part[chunk, :, :, :, :, width:2 * width] = im.reshape(shape)
        core_copies[chunk] = send(
            part.at[chunk, 1 - core], core_in.at[chunk], core_s, core_peer, col, chunk
        )

    def stage_y(chunk):
        core_copies[chunk].wait_recv()
        core_sum[chunk] = part[chunk, core] + core_in[chunk]
        y_copies[chunk] = send(
            core_sum.at[chunk, 1 - yy], y_in.at[chunk], y_s, y_peer, col, chunk
        )

    def stage_z(chunk):
        y_copies[chunk].wait_recv()
        y_sum[chunk] = core_sum[chunk, yy] + y_in[chunk]
        z_copies[chunk] = [
            send(y_sum.at[chunk, z], z_in.at[chunk, d], z_s, row_of(z, yy, core), col, chunk, d)
            for d, z in enumerate(z_hops)
        ]

    def stage_end(chunk):
        total = y_sum[chunk, zz]
        for d, copy in enumerate(z_copies[chunk]):
            copy.wait_recv()
            total = total + z_in[chunk, d]
        reduced[chunk] = total

    for q in range(chunks):
        stage_core(q, tail[0, :, q * span:(q + 1) * span], tail[1, :, q * span:(q + 1) * span])

    count = sources.shape[3]
    selector = (
        lax.broadcasted_iota(jnp.int32, (count, tail.shape[2]), 0) == station[...]
    ).astype(jnp.float32).astype(jnp.bfloat16)
    flat = sources[...].reshape(kinds * local, count)
    if lanes > kinds * local:
        flat = jnp.concatenate(
            [flat, jnp.zeros((lanes - kinds * local, count), jnp.float32)], axis=0
        )
    first, rest = split_two(flat)
    rest = flat - first.astype(jnp.float32)
    second, third = split_two(rest)
    taken = dot_tn(selector, jnp.transpose(first)) + dot_tn(selector, jnp.transpose(second))
    taken = taken + dot_tn(selector, jnp.transpose(third))
    for q in range(chunks):
        adj_out[:, q] = taken[q * span:(q + 1) * span].reshape(rows, 8, lanes)
    adj_copies = [
        send(adj_out.at[slot_of(peer)], adj_in.at[row], adj_s, peer, col, d)
        for d, peer in enumerate(peers)
    ]
    adj_in[row] = adj_out[my_slot]

    for q in range(chunks):
        stage_y(q)
    for d in range(depth - 1):
        bz[d].wait_recv()
        place = blocks.at[row_of(z_from[d], yy, core)]
        by.append(send(place, place, by_s, y_peer, col, d + 1))
        bc.append(send(place, place, bc_s, core_peer, col, d + 1))
    for q in range(chunks):
        stage_z(q)
    for d, z in enumerate([zz] + z_from):
        by[d].wait_recv()
        place = blocks.at[row_of(z, 1 - yy, core)]
        bc.append(send(place, place, bc_s, core_peer, col, depth + d))
    for q in range(chunks):
        stage_end(q)

    for copy in adj_copies:
        copy.wait_recv()
    received = [adj_in[r].reshape(chunks * 8, lanes) for r in range(rows)]
    adjoint = [
        jnp.concatenate([piece[:, n * local:(n + 1) * local] for piece in received], axis=1)
        for n in range(kinds)
    ]

    for q in range(chunks):
        x_copies[q].wait_recv()
        stage_core(chunks + q, rx[q, 0], rx[q, 1])
        if q > 0:
            stage_z(chunks + q - 1)
        stage_y(chunks + q)
    for copy in bc:
        copy.wait_recv()
    stage_z(2 * chunks - 1)
    swaps = []
    for q in range(chunks):
        stage_end(chunks + q)
        swaps.append(send(reduced.at[chunks + q], x_in.at[q], swap_s, row, 1 - col, q))
    for copy in swaps:
        copy.wait_recv()

    own = reduced[0:chunks].reshape(chunks * 8, 2 * width)
    other = x_in[...].reshape(chunks * 8, 2 * width)
    lower = jnp.where(col == 0, own, other)
    upper = jnp.where(col == 0, other, own)
    sums = [
        jnp.concatenate([lower[:, c * width:(c + 1) * width], upper[:, c * width:(c + 1) * width]], axis=1)
        for c in range(2)
    ]

    def block(n):
        return blocks[:, n].reshape(panel, panel)

    count_r = chunks * 8
    rounded = [None] * panels
    solved = [None] * kinds
    for k in range(panels - 1, -1, -1):
        real = sums[0][:, k * panel:(k + 1) * panel]
        imag = sums[1][:, k * panel:(k + 1) * panel]
        for j in range(k + 1, panels):
            place = 2 * kinds + pairs.index((j, k)) * 2
            with_real = dot_nn(rounded[j], block(place))
            with_imag = dot_nn(rounded[j], block(place + 1))
            real = real + with_real[:count_r] + with_imag[count_r:]
            imag = imag + with_real[count_r:] - with_imag[:count_r]
        residue = jnp.concatenate([adjoint[k * 2] - real, adjoint[k * 2 + 1] - imag], axis=0)
        high, low = split_two(residue)
        both = jnp.concatenate([high, low], axis=0)
        products = []
        for c in range(2):
            wide = dot_nt(both, block(k * 2 + c))
            fine = dot_nt(high, block(kinds + k * 2 + c))
            products.append(wide[:2 * count_r] + wide[2 * count_r:] + fine)
        solved[k * 2] = products[0][:count_r] - products[1][count_r:]
        solved[k * 2 + 1] = products[0][count_r:] + products[1][:count_r]
        rounded[k] = jnp.concatenate([solved[k * 2], solved[k * 2 + 1]], axis=0).astype(jnp.bfloat16)
    filler = [jnp.zeros((count_r, lanes - kinds * local), jnp.float32)] if lanes > kinds * local else []
    for r in range(rows):
        pieces = [value[:, r * local:(r + 1) * local] for value in solved] + filler
        sol_out[r] = jnp.concatenate(pieces, axis=1).reshape(chunks, 8, lanes)
    sol_copies = [
        send(sol_out.at[peer], out.at[my_slot], sol_s, peer, col, d)
        for d, peer in enumerate(peers)
    ]
    out[my_slot] = sol_out[row]
    for copy in sol_copies:
        copy.wait_recv()
    for copy in pending:
        copy.wait_send()


def fused_shards(rows, tail_factor, tail_solution, coupling, inverse_blocks, sources, station_map):
    panels, _, local, panel = inverse_blocks.shape
    depth = rows // 4
    width = tail_factor.shape[2]
    rhs = tail_solution.shape[2]
    tall = tail_solution.shape[1]
    chunks = rhs // (rows * 8)
    lanes = -(-panels * 2 * local // 128) * 128
    kept = 4 * panels + panels * (panels - 1)
    vmem = pl.BlockSpec(memory_space=pltpu.VMEM)
    f32, bf16 = jnp.float32, jnp.bfloat16
    sem = pltpu.SemaphoreType.DMA
    gathered = pl.pallas_call(
        functools.partial(fused_kernel, rows, depth, panels, chunks),
        out_shape=jax.ShapeDtypeStruct((rows, chunks, 8, lanes), f32),
        in_specs=[vmem] * 6,
        out_specs=vmem,
        scratch_shapes=[
            pltpu.VMEM((chunks, 2, tall, rows * 8), bf16),
            pltpu.VMEM((2 * chunks, 2, 2, depth, 8, 2 * width), f32),
            pltpu.VMEM((2 * chunks, 2, depth, 8, 2 * width), f32),
            pltpu.VMEM((2 * chunks, 2, depth, 8, 2 * width), f32),
            pltpu.VMEM((2 * chunks, depth, 8, 2 * width), f32),
            pltpu.VMEM((2 * chunks, depth, 8, 2 * width), f32),
            pltpu.VMEM((2 * chunks, depth - 1, 8, 2 * width), f32),
            pltpu.VMEM((2 * chunks, 8, 2 * width), f32),
            pltpu.VMEM((chunks, 8, 2 * width), f32),
            pltpu.VMEM((rows, kept, local, panel), bf16),
            pltpu.VMEM((rows, chunks, 8, lanes), f32),
            pltpu.VMEM((rows, chunks, 8, lanes), f32),
            pltpu.VMEM((rows, chunks, 8, lanes), f32),
            sem((2, chunks)),
            sem((2, rows - 1)),
            sem((2, rows - 1)),
            sem((2, 2 * chunks)),
            sem((2, 2 * chunks)),
            sem((2, 2 * chunks, depth - 1)),
            sem((2, chunks)),
            sem((2, depth - 1)),
            sem((2, depth)),
            sem((2, 2 * depth)),
        ],
        compiler_params=pltpu.CompilerParams(
            collective_id=0, has_side_effects=True, vmem_limit_bytes=40 * 1024 * 1024
        ),
    )(tail_factor, tail_solution, coupling, inverse_blocks, sources, station_map[None, :])
    used = gathered[..., : panels * 2 * local].reshape(rows, chunks, 8, panels, 2, local)
    return jnp.transpose(used, (3, 4, 5, 1, 0, 2)).reshape(panels, 2, local, rhs)


def plan(mesh):
    rows, cols = mesh.shape["row"], mesh.shape["col"]

    def body(tail_factor, tail_solution, coupling, inverse_blocks, sources, station_map):
        fits = (
            cols == 2
            and rows % 4 == 0
            and rows >= 8
            and tail_factor.shape[2] % 128 == 0
            and (rows * 8) % 128 == 0
            and tail_solution.shape[2] % (rows * 8) == 0
            and inverse_blocks.shape[2] % 16 == 0
            and inverse_blocks.shape[3] % 128 == 0
        )
        arrays = (tail_factor, tail_solution, coupling, inverse_blocks, sources, station_map)
        return fused_shards(rows, *arrays) if fits else shards(*arrays)

    return body


def solution(mesh):
    placed = (
        P(None, "row", "col"),
        P(None, "row", "col"),
        P(None, None, "row", None),
        P(None, None, "row", None),
        P(None, None, "row", None),
        P("col"),
    )
    return jax.shard_map(
        plan(mesh), mesh=mesh, in_specs=placed, out_specs=P(None, None, "row", "col"), check_vma=False
    )
```

```python
import functools

import jax
import jax.numpy as jnp
from jax import lax
from jax.experimental import pallas as pl
from jax.experimental.pallas import tpu as pltpu
from jax.sharding import PartitionSpec as P

MESH = pl.DeviceIdType.MESH


def conj_tproduct(factor_part, solution_part):
    real_part = jnp.einsum(
        "pq,pr->qr", factor_part[0], solution_part[0], preferred_element_type=jnp.float32
    ) + jnp.einsum(
        "pq,pr->qr", factor_part[1], solution_part[1], preferred_element_type=jnp.float32
    )
    imag_part = jnp.einsum(
        "pq,pr->qr", factor_part[0], solution_part[1], preferred_element_type=jnp.float32
    ) - jnp.einsum(
        "pq,pr->qr", factor_part[1], solution_part[0], preferred_element_type=jnp.float32
    )
    return jnp.stack([real_part, imag_part])


def complex_product(matrix, vectors):
    high = lax.Precision.HIGHEST
    real_part = jnp.dot(matrix[0], vectors[0], precision=high) - jnp.dot(
        matrix[1], vectors[1], precision=high
    )
    imag_part = jnp.dot(matrix[0], vectors[1], precision=high) + jnp.dot(
        matrix[1], vectors[0], precision=high
    )
    return jnp.stack([real_part, imag_part])


def shards(tail_factor, tail_solution, coupling, inverse_blocks, sources, station_map):
    panel_count = coupling.shape[0]
    panel_width = inverse_blocks.shape[3]
    local_rows = inverse_blocks.shape[2]
    rhs_local = tail_solution.shape[2]
    source_count = sources.shape[3]
    selector = (
        lax.broadcasted_iota(jnp.int32, (source_count, rhs_local), 0) == station_map[None, :]
    ).astype(jnp.float32)
    adjoint_rhs = jnp.einsum("kcps,sr->kcpr", sources, selector, precision=lax.Precision.HIGHEST)
    partial_value = conj_tproduct(
        lax.all_gather(tail_factor, "col", axis=2, tiled=True), tail_solution
    )
    partial_value = partial_value.reshape(2, panel_count, panel_width, rhs_local)
    solved = [None] * panel_count
    rounded = [None] * panel_count
    row_offset = lax.axis_index("row") * local_rows
    own_rhs = jnp.transpose(adjoint_rhs, (1, 0, 2, 3))
    placed_all = lax.dynamic_update_slice_in_dim(
        jnp.zeros_like(partial_value), own_rhs, row_offset, 2
    )
    base_rhs = lax.psum(placed_all - partial_value, "row")
    whole_coupling = lax.all_gather(coupling, "row", axis=2, tiled=True)
    gathered = [None] * panel_count
    for panel_index in range(panel_count - 1, -1, -1):
        full_y = base_rhs[:, panel_index]
        for later_panel in range(panel_index + 1, panel_count):
            block_cols = whole_coupling[later_panel][
                :, :, panel_index * panel_width : (panel_index + 1) * panel_width
            ]
            full_y = full_y - conj_tproduct(block_cols, gathered[later_panel])
        solved[panel_index] = complex_product(inverse_blocks[panel_index], full_y)
        rounded[panel_index] = solved[panel_index].astype(jnp.bfloat16)
        if panel_index > 0:
            gathered[panel_index] = lax.all_gather(rounded[panel_index], "row", axis=1, tiled=True)
    return jnp.stack(solved)


def split_two(value):
    high = value.astype(jnp.bfloat16)
    low = (value - high.astype(jnp.float32)).astype(jnp.bfloat16)
    return high, low


def dot_tn(left, right):
    return lax.dot_general(
        left, right, (((0,), (0,)), ((), ())), preferred_element_type=jnp.float32
    )


def dot_nt(left, right):
    return lax.dot_general(
        left, right, (((1,), (1,)), ((), ())), preferred_element_type=jnp.float32
    )


def dot_nn(left, right):
    return lax.dot_general(
        left, right, (((1,), (0,)), ((), ())), preferred_element_type=jnp.float32
    )


def panel_pairs(panels):
    return [(j, k) for j in range(panels) for k in range(j)]


def fused_kernel(
    rows, depth, panels, chunks,
    factor_h, tail_h, coupling_h, inverse_h, sources_h, station_h, out,
    factor, tail, coupling, inverse, sources, station, rx, part, core_in, core_sum, y_in, y_sum, z_in, reduced, far_in,
    blocks, adj_out, adj_in, sol_out, xs, adj_s, sol_s, core_s, y_s, z_s, far_s,
    bz_s, by_s, bc_s, load_s,
):
    row = lax.axis_index("row")
    col = lax.axis_index("col")
    core = lax.rem(row, 2)
    yy = lax.rem(row // 2, 2)
    zz = row // 4
    width = factor.shape[2]
    local = inverse.shape[2]
    panel = inverse.shape[3]
    span = rows * 8
    lanes = adj_in.shape[3]
    kinds = panels * 2

    def slot_of(r):
        return (lax.rem(r, 2) * 2 + lax.rem(r // 2, 2)) * depth + r // 4

    def row_of(z, y, c):
        return z * 4 + y * 2 + c

    my_slot = slot_of(row)
    peers = [lax.rem(row + d, rows) for d in range(1, rows)]
    core_peer = row_of(zz, yy, 1 - core)
    y_peer = row_of(zz, 1 - yy, core)
    z_hops = [lax.rem(zz + d, depth) for d in range(1, depth)]
    z_from = [lax.rem(zz + depth - d, depth) for d in range(1, depth)]
    pending = []

    def send(source, target, sems, device_row, device_col, *index):
        copy = pltpu.make_async_remote_copy(
            src_ref=source, dst_ref=target,
            send_sem=sems.at[(0, *index)], recv_sem=sems.at[(1, *index)],
            device_id=(device_row, device_col), device_id_type=MESH,
        )
        copy.start()
        pending.append(copy)
        return copy

    loads = []
    for n, (source, target) in enumerate((
        (inverse_h, inverse), (coupling_h, coupling), (tail_h, tail),
        (factor_h, factor), (sources_h, sources), (station_h, station),
    )):
        load = pltpu.make_async_copy(source, target, load_s.at[n])
        load.start()
        loads.append(load)
    barrier = pltpu.get_barrier_semaphore()
    for peer in peers:
        pl.semaphore_signal(barrier, inc=1, device_id=(peer, col), device_id_type=MESH)
    for z in [zz] + z_hops:
        pl.semaphore_signal(
            barrier, inc=1, device_id=(row_of(z, yy, core), 1 - col), device_id_type=MESH
        )

    loads[0].wait()
    loads[1].wait()
    pairs = panel_pairs(panels)
    for k in range(panels):
        for c in range(2):
            high, low = split_two(inverse[k, c])
            blocks[row, k * 2 + c] = high
            blocks[row, kinds + k * 2 + c] = low
    for place, (j, k) in enumerate(pairs):
        for c in range(2):
            blocks[row, 2 * kinds + place * 2 + c] = coupling[
                j, c, :, k * panel:(k + 1) * panel
            ]
    pl.semaphore_wait(barrier, rows - 1 + depth)

    def send_x(q):
        return send(tail_h.at[:, :, pl.ds(q * span, span)], rx.at[q], xs, row, 1 - col, q)

    x_copies = [send_x(0)]

    bz = [
        send(blocks.at[row], blocks.at[row], bz_s, row_of(z, yy, core), col, d)
        for d, z in enumerate(z_hops)
    ]
    by = [send(blocks.at[row], blocks.at[row], by_s, y_peer, col, 0)]
    bc = [send(blocks.at[row], blocks.at[row], bc_s, core_peer, col, 0)]

    def multiply(real, imag):
        re = dot_tn(real, factor[0]) + dot_tn(imag, factor[1])
        im = dot_tn(imag, factor[0]) - dot_tn(real, factor[1])
        return re, im

    core_copies, y_copies, z_copies = {}, {}, {}

    def stage_core(chunk, real, imag):
        re, im = multiply(real, imag)
        shape = (2, 2, depth, 8, width)
        part[chunk, :, :, :, :, 0:width] = re.reshape(shape)
        part[chunk, :, :, :, :, width:2 * width] = im.reshape(shape)
        core_copies[chunk] = send(
            part.at[chunk, 1 - core], core_in.at[chunk], core_s, core_peer, col, chunk
        )

    def stage_y(chunk):
        core_copies[chunk].wait_recv()
        core_sum[chunk] = part[chunk, core] + core_in[chunk]
        y_copies[chunk] = send(
            core_sum.at[chunk, 1 - yy], y_in.at[chunk], y_s, y_peer, col, chunk
        )

    def stage_z(chunk):
        y_copies[chunk].wait_recv()
        y_sum[chunk] = core_sum[chunk, yy] + y_in[chunk]
        if chunk >= chunks:
            z_copies[chunk] = [
                send(
                    y_sum.at[chunk, z], far_in.at[chunk - chunks, d], far_s,
                    row_of(z, yy, core), 1 - col, chunk - chunks, d,
                )
                for d, z in enumerate([zz] + z_hops)
            ]
            return
        z_copies[chunk] = [
            send(y_sum.at[chunk, z], z_in.at[chunk, d], z_s, row_of(z, yy, core), col, chunk, d)
            for d, z in enumerate(z_hops)
        ]

    def stage_end(chunk):
        total = y_sum[chunk, zz]
        for d, copy in enumerate(z_copies[chunk]):
            copy.wait_recv()
            total = total + z_in[chunk, d]
        reduced[chunk] = total

    loads[2].wait()
    loads[3].wait()
    for q in range(chunks):
        stage_core(q, tail[0, :, q * span:(q + 1) * span], tail[1, :, q * span:(q + 1) * span])

    loads[4].wait()
    loads[5].wait()
    count = sources.shape[3]
    selector = (
        lax.broadcasted_iota(jnp.int32, (count, tail.shape[2]), 0) == station[...]
    ).astype(jnp.float32).astype(jnp.bfloat16)
    flat = sources[...].reshape(kinds * local, count)
    if lanes > kinds * local:
        flat = jnp.concatenate(
            [flat, jnp.zeros((lanes - kinds * local, count), jnp.float32)], axis=0
        )
    first, rest = split_two(flat)
    rest = flat - first.astype(jnp.float32)
    second, third = split_two(rest)
    taken = dot_tn(selector, jnp.transpose(first)) + dot_tn(selector, jnp.transpose(second))
    taken = taken + dot_tn(selector, jnp.transpose(third))
    for q in range(chunks):
        adj_out[:, q] = taken[q * span:(q + 1) * span].reshape(rows, 8, lanes)
    adj_copies = [
        send(adj_out.at[slot_of(peer)], adj_in.at[row], adj_s, peer, col, d)
        for d, peer in enumerate(peers)
    ]
    adj_in[row] = adj_out[my_slot]

    x_copies += [send_x(q) for q in range(1, chunks)]
    for q in range(chunks):
        stage_y(q)
    for d in range(depth - 1):
        bz[d].wait_recv()
        place = blocks.at[row_of(z_from[d], yy, core)]
        by.append(send(place, place, by_s, y_peer, col, d + 1))
        bc.append(send(place, place, bc_s, core_peer, col, d + 1))
    for q in range(chunks):
        stage_z(q)

    for q in range(chunks):
        x_copies[q].wait_recv()
        stage_core(chunks + q, rx[q, 0], rx[q, 1])
        if q == 0:
            for own_chunk in range(chunks):
                stage_end(own_chunk)
        stage_y(chunks + q)
        stage_z(chunks + q)
        if q == 0:
            for copy in adj_copies:
                copy.wait_recv()
            received = [adj_in[r].reshape(chunks * 8, lanes) for r in range(rows)]
            adjoint = [
                jnp.concatenate(
                    [piece[:, n * local:(n + 1) * local] for piece in received], axis=1
                )
                for n in range(kinds)
            ]
            for d, z in enumerate([zz] + z_from):
                by[d].wait_recv()
                place = blocks.at[row_of(z, 1 - yy, core)]
                bc.append(send(place, place, bc_s, core_peer, col, depth + d))
    for copy in bc:
        copy.wait_recv()
    others = []
    for q in range(chunks):
        total = None
        for d, copy in enumerate(z_copies[chunks + q]):
            copy.wait_recv()
            total = far_in[q, d] if total is None else total + far_in[q, d]
        others.append(total)

    own = reduced[0:chunks].reshape(chunks * 8, 2 * width)
    other = jnp.concatenate(others, axis=0)
    lower = jnp.where(col == 0, own, other)
    upper = jnp.where(col == 0, other, own)
    sums = [
        jnp.concatenate([lower[:, c * width:(c + 1) * width], upper[:, c * width:(c + 1) * width]], axis=1)
        for c in range(2)
    ]

    def block(n):
        return blocks[:, n].reshape(panel, panel)

    count_r = chunks * 8
    rounded = [None] * panels
    solved = [None] * kinds
    for k in range(panels - 1, -1, -1):
        real = sums[0][:, k * panel:(k + 1) * panel]
        imag = sums[1][:, k * panel:(k + 1) * panel]
        for j in range(k + 1, panels):
            place = 2 * kinds + pairs.index((j, k)) * 2
            with_real = dot_nn(rounded[j], block(place))
            with_imag = dot_nn(rounded[j], block(place + 1))
            real = real + with_real[:count_r] + with_imag[count_r:]
            imag = imag + with_real[count_r:] - with_imag[:count_r]
        residue = jnp.concatenate([adjoint[k * 2] - real, adjoint[k * 2 + 1] - imag], axis=0)
        high, low = split_two(residue)
        both = jnp.concatenate([high, low], axis=0)
        products = []
        for c in range(2):
            wide = dot_nt(both, block(k * 2 + c))
            fine = dot_nt(high, block(kinds + k * 2 + c))
            products.append(wide[:2 * count_r] + wide[2 * count_r:] + fine)
        solved[k * 2] = products[0][:count_r] - products[1][count_r:]
        solved[k * 2 + 1] = products[0][count_r:] + products[1][:count_r]
        rounded[k] = jnp.concatenate([solved[k * 2], solved[k * 2 + 1]], axis=0).astype(jnp.bfloat16)
    filler = [jnp.zeros((count_r, lanes - kinds * local), jnp.float32)] if lanes > kinds * local else []
    for r in range(rows):
        pieces = [value[:, r * local:(r + 1) * local] for value in solved] + filler
        sol_out[r] = jnp.concatenate(pieces, axis=1).reshape(chunks, 8, lanes)
    sol_copies = [
        send(sol_out.at[peer], out.at[my_slot], sol_s, peer, col, d)
        for d, peer in enumerate(peers)
    ]
    out[my_slot] = sol_out[row]
    for copy in sol_copies:
        copy.wait_recv()
    for copy in pending:
        copy.wait_send()


def fused_shards(rows, tail_factor, tail_solution, coupling, inverse_blocks, sources, station_map):
    panels, _, local, panel = inverse_blocks.shape
    depth = rows // 4
    width = tail_factor.shape[2]
    rhs = tail_solution.shape[2]
    tall = tail_solution.shape[1]
    chunks = rhs // (rows * 8)
    lanes = -(-panels * 2 * local // 128) * 128
    kept = 4 * panels + panels * (panels - 1)
    vmem = pl.BlockSpec(memory_space=pltpu.VMEM)
    f32, bf16 = jnp.float32, jnp.bfloat16
    sem = pltpu.SemaphoreType.DMA
    gathered = pl.pallas_call(
        functools.partial(fused_kernel, rows, depth, panels, chunks),
        out_shape=jax.ShapeDtypeStruct((rows, chunks, 8, lanes), f32),
        in_specs=[pl.BlockSpec(memory_space=pltpu.HBM)] * 6,
        out_specs=vmem,
        scratch_shapes=[
            pltpu.VMEM(tail_factor.shape, bf16),
            pltpu.VMEM(tail_solution.shape, bf16),
            pltpu.VMEM(coupling.shape, bf16),
            pltpu.VMEM(inverse_blocks.shape, f32),
            pltpu.VMEM(sources.shape, f32),
            pltpu.VMEM((1, rhs), jnp.int32),
            pltpu.VMEM((chunks, 2, tall, rows * 8), bf16),
            pltpu.VMEM((2 * chunks, 2, 2, depth, 8, 2 * width), f32),
            pltpu.VMEM((2 * chunks, 2, depth, 8, 2 * width), f32),
            pltpu.VMEM((2 * chunks, 2, depth, 8, 2 * width), f32),
            pltpu.VMEM((2 * chunks, depth, 8, 2 * width), f32),
            pltpu.VMEM((2 * chunks, depth, 8, 2 * width), f32),
            pltpu.VMEM((chunks, depth - 1, 8, 2 * width), f32),
            pltpu.VMEM((chunks, 8, 2 * width), f32),
            pltpu.VMEM((chunks, depth, 8, 2 * width), f32),
            pltpu.VMEM((rows, kept, local, panel), bf16),
            pltpu.VMEM((rows, chunks, 8, lanes), f32),
            pltpu.VMEM((rows, chunks, 8, lanes), f32),
            pltpu.VMEM((rows, chunks, 8, lanes), f32),
            sem((2, chunks)),
            sem((2, rows - 1)),
            sem((2, rows - 1)),
            sem((2, 2 * chunks)),
            sem((2, 2 * chunks)),
            sem((2, chunks, depth - 1)),
            sem((2, chunks, depth)),
            sem((2, depth - 1)),
            sem((2, depth)),
            sem((2, 2 * depth)),
            sem((6,)),
        ],
        compiler_params=pltpu.CompilerParams(
            collective_id=0, has_side_effects=True, vmem_limit_bytes=63 * 1024 * 1024
        ),
    )(tail_factor, tail_solution, coupling, inverse_blocks, sources, station_map[None, :])
    used = gathered[..., : panels * 2 * local].reshape(rows, chunks, 8, panels, 2, local)
    return jnp.transpose(used, (3, 4, 5, 1, 0, 2)).reshape(panels, 2, local, rhs)


def plan(mesh):
    rows, cols = mesh.shape["row"], mesh.shape["col"]

    def body(tail_factor, tail_solution, coupling, inverse_blocks, sources, station_map):
        fits = (
            cols == 2
            and rows % 4 == 0
            and rows >= 8
            and tail_factor.shape[2] % 128 == 0
            and (rows * 8) % 128 == 0
            and tail_solution.shape[2] % (rows * 8) == 0
            and inverse_blocks.shape[2] % 16 == 0
            and inverse_blocks.shape[3] % 128 == 0
        )
        arrays = (tail_factor, tail_solution, coupling, inverse_blocks, sources, station_map)
        return fused_shards(rows, *arrays) if fits else shards(*arrays)

    return body


def solution(mesh):
    placed = (
        P(None, "row", "col"),
        P(None, "row", "col"),
        P(None, None, "row", None),
        P(None, None, "row", None),
        P(None, None, "row", None),
        P("col"),
    )
    return jax.shard_map(
        plan(mesh), mesh=mesh, in_specs=placed, out_specs=P(None, None, "row", "col"), check_vma=False
    )
```

```python
import functools

import jax
import jax.numpy as jnp
from jax import lax
from jax.experimental import pallas as pl
from jax.experimental.pallas import tpu as pltpu
from jax.sharding import PartitionSpec as P

MESH = pl.DeviceIdType.MESH


def conj_tproduct(factor_part, solution_part):
    real_part = jnp.einsum(
        "pq,pr->qr", factor_part[0], solution_part[0], preferred_element_type=jnp.float32
    ) + jnp.einsum(
        "pq,pr->qr", factor_part[1], solution_part[1], preferred_element_type=jnp.float32
    )
    imag_part = jnp.einsum(
        "pq,pr->qr", factor_part[0], solution_part[1], preferred_element_type=jnp.float32
    ) - jnp.einsum(
        "pq,pr->qr", factor_part[1], solution_part[0], preferred_element_type=jnp.float32
    )
    return jnp.stack([real_part, imag_part])


def complex_product(matrix, vectors):
    high = lax.Precision.HIGHEST
    real_part = jnp.dot(matrix[0], vectors[0], precision=high) - jnp.dot(
        matrix[1], vectors[1], precision=high
    )
    imag_part = jnp.dot(matrix[0], vectors[1], precision=high) + jnp.dot(
        matrix[1], vectors[0], precision=high
    )
    return jnp.stack([real_part, imag_part])


def shards(tail_factor, tail_solution, coupling, inverse_blocks, sources, station_map):
    panel_count = coupling.shape[0]
    panel_width = inverse_blocks.shape[3]
    local_rows = inverse_blocks.shape[2]
    rhs_local = tail_solution.shape[2]
    source_count = sources.shape[3]
    selector = (
        lax.broadcasted_iota(jnp.int32, (source_count, rhs_local), 0) == station_map[None, :]
    ).astype(jnp.float32)
    adjoint_rhs = jnp.einsum("kcps,sr->kcpr", sources, selector, precision=lax.Precision.HIGHEST)
    partial_value = conj_tproduct(
        lax.all_gather(tail_factor, "col", axis=2, tiled=True), tail_solution
    )
    partial_value = partial_value.reshape(2, panel_count, panel_width, rhs_local)
    solved = [None] * panel_count
    rounded = [None] * panel_count
    row_offset = lax.axis_index("row") * local_rows
    own_rhs = jnp.transpose(adjoint_rhs, (1, 0, 2, 3))
    placed_all = lax.dynamic_update_slice_in_dim(
        jnp.zeros_like(partial_value), own_rhs, row_offset, 2
    )
    base_rhs = lax.psum(placed_all - partial_value, "row")
    whole_coupling = lax.all_gather(coupling, "row", axis=2, tiled=True)
    gathered = [None] * panel_count
    for panel_index in range(panel_count - 1, -1, -1):
        full_y = base_rhs[:, panel_index]
        for later_panel in range(panel_index + 1, panel_count):
            block_cols = whole_coupling[later_panel][
                :, :, panel_index * panel_width : (panel_index + 1) * panel_width
            ]
            full_y = full_y - conj_tproduct(block_cols, gathered[later_panel])
        solved[panel_index] = complex_product(inverse_blocks[panel_index], full_y)
        rounded[panel_index] = solved[panel_index].astype(jnp.bfloat16)
        if panel_index > 0:
            gathered[panel_index] = lax.all_gather(rounded[panel_index], "row", axis=1, tiled=True)
    return jnp.stack(solved)


def split_two(value):
    high = value.astype(jnp.bfloat16)
    low = (value - high.astype(jnp.float32)).astype(jnp.bfloat16)
    return high, low


def dot_tn(left, right):
    return lax.dot_general(
        left, right, (((0,), (0,)), ((), ())), preferred_element_type=jnp.float32
    )


def dot_nt(left, right):
    return lax.dot_general(
        left, right, (((1,), (1,)), ((), ())), preferred_element_type=jnp.float32
    )


def dot_nn(left, right):
    return lax.dot_general(
        left, right, (((1,), (0,)), ((), ())), preferred_element_type=jnp.float32
    )


def panel_pairs(panels):
    return [(j, k) for j in range(panels) for k in range(j)]


def fused_kernel(
    rows, depth, panels, chunks,
    factor_h, tail_h, coupling_h, inverse_h, sources_h, station_h, out,
    factor, tail, coupling, inverse, sources, station, rx, part, core_in, core_sum, y_in, y_sum, z_in, reduced, far_in,
    core_low, y_low, z_low, sol_in,
    blocks, adj_out, adj_in, sol_out, xs, adj_s, sol_s, core_s, y_s, z_s, far_s,
    bz_s, by_s, bc_s, load_s,
):
    row = lax.axis_index("row")
    col = lax.axis_index("col")
    core = lax.rem(row, 2)
    yy = lax.rem(row // 2, 2)
    zz = row // 4
    width = factor.shape[2]
    local = inverse.shape[2]
    panel = inverse.shape[3]
    span = rows * 8
    lanes = adj_in.shape[3]
    kinds = panels * 2

    def slot_of(r):
        return (lax.rem(r, 2) * 2 + lax.rem(r // 2, 2)) * depth + r // 4

    def row_of(z, y, c):
        return z * 4 + y * 2 + c

    my_slot = slot_of(row)
    peers = [lax.rem(row + d, rows) for d in range(1, rows)]
    core_peer = row_of(zz, yy, 1 - core)
    y_peer = row_of(zz, 1 - yy, core)
    z_hops = [lax.rem(zz + d, depth) for d in range(1, depth)]
    z_from = [lax.rem(zz + depth - d, depth) for d in range(1, depth)]
    pending = []

    def send(source, target, sems, device_row, device_col, *index):
        copy = pltpu.make_async_remote_copy(
            src_ref=source, dst_ref=target,
            send_sem=sems.at[(0, *index)], recv_sem=sems.at[(1, *index)],
            device_id=(device_row, device_col), device_id_type=MESH,
        )
        copy.start()
        pending.append(copy)
        return copy

    loads = []
    for n, (source, target) in enumerate((
        (inverse_h, inverse), (coupling_h, coupling), (tail_h, tail),
        (factor_h, factor), (sources_h, sources), (station_h, station),
    )):
        load = pltpu.make_async_copy(source, target, load_s.at[n])
        load.start()
        loads.append(load)
    barrier = pltpu.get_barrier_semaphore()
    for peer in peers:
        pl.semaphore_signal(barrier, inc=1, device_id=(peer, col), device_id_type=MESH)
    for z in [zz] + z_hops:
        pl.semaphore_signal(
            barrier, inc=1, device_id=(row_of(z, yy, core), 1 - col), device_id_type=MESH
        )

    loads[0].wait()
    loads[1].wait()
    pairs = panel_pairs(panels)
    for k in range(panels):
        for c in range(2):
            high, low = split_two(inverse[k, c])
            blocks[row, k * 2 + c] = high
            blocks[row, kinds + k * 2 + c] = low
    for place, (j, k) in enumerate(pairs):
        for c in range(2):
            blocks[row, 2 * kinds + place * 2 + c] = coupling[
                j, c, :, k * panel:(k + 1) * panel
            ]
    pl.semaphore_wait(barrier, rows - 1 + depth)

    def send_x(q):
        return send(tail_h.at[:, :, pl.ds(q * span, span)], rx.at[q], xs, row, 1 - col, q)

    x_copies = [send_x(0)]

    bz = [
        send(blocks.at[row], blocks.at[row], bz_s, row_of(z, yy, core), col, d)
        for d, z in enumerate(z_hops)
    ]
    by = [send(blocks.at[row], blocks.at[row], by_s, y_peer, col, 0)]
    bc = [send(blocks.at[row], blocks.at[row], bc_s, core_peer, col, 0)]

    def multiply(real, imag):
        re = dot_tn(real, factor[0]) + dot_tn(imag, factor[1])
        im = dot_tn(imag, factor[0]) - dot_tn(real, factor[1])
        return re, im

    core_copies, y_copies, z_copies = {}, {}, {}

    def stage_core(chunk, real, imag):
        re, im = multiply(real, imag)
        shape = (2, 2, depth, 8, width)
        part[chunk, :, :, :, 0:8, :] = re.reshape(shape)
        part[chunk, :, :, :, 8:16, :] = im.reshape(shape)
        core_copies[chunk] = send(
            part.at[chunk, 1 - core], core_in.at[chunk], core_s, core_peer, col, chunk
        )

    def stage_y(chunk):
        core_copies[chunk].wait_recv()
        core_sum[chunk] = part[chunk, core] + core_in[chunk]
        if chunk >= chunks:
            late = chunk - chunks
            core_low[late] = core_sum[chunk, 1 - yy].astype(jnp.bfloat16)
            y_copies[chunk] = send(core_low.at[late], y_low.at[late], y_s, y_peer, col, chunk)
            return
        y_copies[chunk] = send(
            core_sum.at[chunk, 1 - yy], y_in.at[chunk], y_s, y_peer, col, chunk
        )

    def stage_z(chunk):
        y_copies[chunk].wait_recv()
        if chunk >= chunks:
            late = chunk - chunks
            z_low[late] = (core_sum[chunk, yy] + y_low[late].astype(jnp.float32)).astype(jnp.bfloat16)
            z_copies[chunk] = [
                send(
                    z_low.at[late, z], far_in.at[late, d], far_s,
                    row_of(z, yy, core), 1 - col, late, d,
                )
                for d, z in enumerate([zz] + z_hops)
            ]
            return
        y_sum[chunk] = core_sum[chunk, yy] + y_in[chunk]
        z_copies[chunk] = [
            send(y_sum.at[chunk, z], z_in.at[chunk, d], z_s, row_of(z, yy, core), col, chunk, d)
            for d, z in enumerate(z_hops)
        ]

    def stage_end(chunk):
        total = y_sum[chunk, zz]
        for d, copy in enumerate(z_copies[chunk]):
            copy.wait_recv()
            total = total + z_in[chunk, d]
        reduced[chunk] = total

    loads[2].wait()
    loads[3].wait()
    for q in range(chunks):
        stage_core(q, tail[0, :, q * span:(q + 1) * span], tail[1, :, q * span:(q + 1) * span])

    loads[4].wait()
    loads[5].wait()
    count = sources.shape[3]
    selector = (
        lax.broadcasted_iota(jnp.int32, (count, tail.shape[2]), 0) == station[...]
    ).astype(jnp.float32).astype(jnp.bfloat16)
    flat = sources[...].reshape(kinds * local, count)
    if lanes > kinds * local:
        flat = jnp.concatenate(
            [flat, jnp.zeros((lanes - kinds * local, count), jnp.float32)], axis=0
        )
    first, rest = split_two(flat)
    rest = flat - first.astype(jnp.float32)
    second, third = split_two(rest)
    taken = dot_tn(selector, jnp.transpose(first)) + dot_tn(selector, jnp.transpose(second))
    taken = taken + dot_tn(selector, jnp.transpose(third))
    for q in range(chunks):
        adj_out[:, q] = taken[q * span:(q + 1) * span].reshape(rows, 8, lanes)
    adj_copies = [
        send(adj_out.at[slot_of(peer)], adj_in.at[row], adj_s, peer, col, d)
        for d, peer in enumerate(peers)
    ]
    adj_in[row] = adj_out[my_slot]

    x_copies += [send_x(q) for q in range(1, chunks)]
    for q in range(chunks):
        stage_y(q)
    for d in range(depth - 1):
        bz[d].wait_recv()
        place = blocks.at[row_of(z_from[d], yy, core)]
        by.append(send(place, place, by_s, y_peer, col, d + 1))
        bc.append(send(place, place, bc_s, core_peer, col, d + 1))
    for q in range(chunks):
        stage_z(q)

    for q in range(chunks):
        x_copies[q].wait_recv()
        stage_core(chunks + q, rx[q, 0], rx[q, 1])
        if q == 0:
            for own_chunk in range(chunks):
                stage_end(own_chunk)
        stage_y(chunks + q)
        stage_z(chunks + q)
        if q == 0:
            for copy in adj_copies:
                copy.wait_recv()
            received = [adj_in[r].reshape(chunks * 8, lanes) for r in range(rows)]
            adjoint = [
                jnp.concatenate(
                    [piece[:, n * local:(n + 1) * local] for piece in received], axis=1
                )
                for n in range(kinds)
            ]
            for d, z in enumerate([zz] + z_from):
                by[d].wait_recv()
                place = blocks.at[row_of(z, 1 - yy, core)]
                bc.append(send(place, place, bc_s, core_peer, col, depth + d))
    for copy in bc:
        copy.wait_recv()
    others = []
    for q in range(chunks):
        total = None
        for d, copy in enumerate(z_copies[chunks + q]):
            copy.wait_recv()
            piece = far_in[q, d].astype(jnp.float32)
            total = piece if total is None else total + piece
        others.append(total)

    owns = [reduced[q] for q in range(chunks)]
    sums = []
    for c in range(2):
        own = jnp.concatenate([value[c * 8:(c + 1) * 8] for value in owns], axis=0)
        other = jnp.concatenate([value[c * 8:(c + 1) * 8] for value in others], axis=0)
        lower = jnp.where(col == 0, own, other)
        upper = jnp.where(col == 0, other, own)
        sums.append(jnp.concatenate([lower, upper], axis=1))

    def block(n):
        return blocks[:, n].reshape(panel, panel)

    count_r = chunks * 8
    rounded = [None] * panels
    solved = [None] * kinds
    for k in range(panels - 1, -1, -1):
        real = sums[0][:, k * panel:(k + 1) * panel]
        imag = sums[1][:, k * panel:(k + 1) * panel]
        for j in range(k + 1, panels):
            place = 2 * kinds + pairs.index((j, k)) * 2
            with_real = dot_nn(rounded[j], block(place))
            with_imag = dot_nn(rounded[j], block(place + 1))
            real = real + with_real[:count_r] + with_imag[count_r:]
            imag = imag + with_real[count_r:] - with_imag[:count_r]
        residue = jnp.concatenate([adjoint[k * 2] - real, adjoint[k * 2 + 1] - imag], axis=0)
        high, low = split_two(residue)
        both = jnp.concatenate([high, low], axis=0)
        products = []
        for c in range(2):
            wide = dot_nt(both, block(k * 2 + c))
            fine = dot_nt(high, block(kinds + k * 2 + c))
            products.append(wide[:2 * count_r] + wide[2 * count_r:] + fine)
        solved[k * 2] = products[0][:count_r] - products[1][count_r:]
        solved[k * 2 + 1] = products[0][count_r:] + products[1][:count_r]
        rounded[k] = jnp.concatenate([solved[k * 2], solved[k * 2 + 1]], axis=0).astype(jnp.bfloat16)
    filler = [jnp.zeros((count_r, lanes - kinds * local), jnp.float32)] if lanes > kinds * local else []
    for r in range(rows):
        pieces = [value[:, r * local:(r + 1) * local] for value in solved] + filler
        sol_out[r] = jnp.concatenate(pieces, axis=1).astype(jnp.bfloat16)
    sol_copies = [
        send(sol_out.at[peer], sol_in.at[my_slot], sol_s, peer, col, d)
        for d, peer in enumerate(peers)
    ]
    sol_in[my_slot] = sol_out[row]
    for copy in sol_copies:
        copy.wait_recv()
    found = sol_in[...].astype(jnp.float32)
    for q in range(chunks):
        turned = jnp.transpose(found[:, q * 8:(q + 1) * 8].reshape(span, lanes))
        out[:, :, :, q * span:(q + 1) * span] = turned[:kinds * local].reshape(
            panels, 2, local, span
        )
    for copy in pending:
        copy.wait_send()


def fused_shards(rows, tail_factor, tail_solution, coupling, inverse_blocks, sources, station_map):
    panels, _, local, panel = inverse_blocks.shape
    depth = rows // 4
    width = tail_factor.shape[2]
    rhs = tail_solution.shape[2]
    tall = tail_solution.shape[1]
    chunks = rhs // (rows * 8)
    lanes = -(-panels * 2 * local // 128) * 128
    kept = 4 * panels + panels * (panels - 1)
    vmem = pl.BlockSpec(memory_space=pltpu.VMEM)
    f32, bf16 = jnp.float32, jnp.bfloat16
    sem = pltpu.SemaphoreType.DMA
    return pl.pallas_call(
        functools.partial(fused_kernel, rows, depth, panels, chunks),
        out_shape=jax.ShapeDtypeStruct((panels, 2, local, rhs), f32),
        in_specs=[pl.BlockSpec(memory_space=pltpu.HBM)] * 6,
        out_specs=vmem,
        scratch_shapes=[
            pltpu.VMEM(tail_factor.shape, bf16),
            pltpu.VMEM(tail_solution.shape, bf16),
            pltpu.VMEM(coupling.shape, bf16),
            pltpu.VMEM(inverse_blocks.shape, f32),
            pltpu.VMEM(sources.shape, f32),
            pltpu.VMEM((1, rhs), jnp.int32),
            pltpu.VMEM((chunks, 2, tall, rows * 8), bf16),
            pltpu.VMEM((2 * chunks, 2, 2, depth, 16, width), f32),
            pltpu.VMEM((2 * chunks, 2, depth, 16, width), f32),
            pltpu.VMEM((2 * chunks, 2, depth, 16, width), f32),
            pltpu.VMEM((chunks, depth, 16, width), f32),
            pltpu.VMEM((chunks, depth, 16, width), f32),
            pltpu.VMEM((chunks, depth - 1, 16, width), f32),
            pltpu.VMEM((chunks, 16, width), f32),
            pltpu.VMEM((chunks, depth, 16, width), bf16),
            pltpu.VMEM((chunks, depth, 16, width), bf16),
            pltpu.VMEM((chunks, depth, 16, width), bf16),
            pltpu.VMEM((chunks, depth, 16, width), bf16),
            pltpu.VMEM((rows, chunks * 8, lanes), bf16),
            pltpu.VMEM((rows, kept, local, panel), bf16),
            pltpu.VMEM((rows, chunks, 8, lanes), f32),
            pltpu.VMEM((rows, chunks, 8, lanes), f32),
            pltpu.VMEM((rows, chunks * 8, lanes), bf16),
            sem((2, chunks)),
            sem((2, rows - 1)),
            sem((2, rows - 1)),
            sem((2, 2 * chunks)),
            sem((2, 2 * chunks)),
            sem((2, chunks, depth - 1)),
            sem((2, chunks, depth)),
            sem((2, depth - 1)),
            sem((2, depth)),
            sem((2, 2 * depth)),
            sem((6,)),
        ],
        compiler_params=pltpu.CompilerParams(
            collective_id=0, has_side_effects=True, vmem_limit_bytes=63 * 1024 * 1024
        ),
    )(tail_factor, tail_solution, coupling, inverse_blocks, sources, station_map[None, :])


def plan(mesh):
    rows, cols = mesh.shape["row"], mesh.shape["col"]

    def body(tail_factor, tail_solution, coupling, inverse_blocks, sources, station_map):
        fits = (
            cols == 2
            and rows % 4 == 0
            and rows >= 8
            and tail_factor.shape[2] % 128 == 0
            and (rows * 8) % 128 == 0
            and tail_solution.shape[2] % (rows * 16) == 0
            and inverse_blocks.shape[2] % 16 == 0
            and inverse_blocks.shape[3] % 128 == 0
        )
        arrays = (tail_factor, tail_solution, coupling, inverse_blocks, sources, station_map)
        return fused_shards(rows, *arrays) if fits else shards(*arrays)

    return body


def solution(mesh):
    placed = (
        P(None, "row", "col"),
        P(None, "row", "col"),
        P(None, None, "row", None),
        P(None, None, "row", None),
        P(None, None, "row", None),
        P("col"),
    )
    return jax.shard_map(
        plan(mesh), mesh=mesh, in_specs=placed, out_specs=P(None, None, "row", "col"), check_vma=False
    )
```

```python
import functools

import jax
import jax.numpy as jnp
from jax import lax
from jax.experimental import pallas as pl
from jax.experimental.pallas import tpu as pltpu
from jax.sharding import PartitionSpec as P

MESH = pl.DeviceIdType.MESH


def conj_tproduct(factor_part, solution_part):
    real_part = jnp.einsum(
        "pq,pr->qr", factor_part[0], solution_part[0], preferred_element_type=jnp.float32
    ) + jnp.einsum(
        "pq,pr->qr", factor_part[1], solution_part[1], preferred_element_type=jnp.float32
    )
    imag_part = jnp.einsum(
        "pq,pr->qr", factor_part[0], solution_part[1], preferred_element_type=jnp.float32
    ) - jnp.einsum(
        "pq,pr->qr", factor_part[1], solution_part[0], preferred_element_type=jnp.float32
    )
    return jnp.stack([real_part, imag_part])


def complex_product(matrix, vectors):
    high = lax.Precision.HIGHEST
    real_part = jnp.dot(matrix[0], vectors[0], precision=high) - jnp.dot(
        matrix[1], vectors[1], precision=high
    )
    imag_part = jnp.dot(matrix[0], vectors[1], precision=high) + jnp.dot(
        matrix[1], vectors[0], precision=high
    )
    return jnp.stack([real_part, imag_part])


def shards(tail_factor, tail_solution, coupling, inverse_blocks, sources, station_map):
    panel_count = coupling.shape[0]
    panel_width = inverse_blocks.shape[3]
    local_rows = inverse_blocks.shape[2]
    rhs_local = tail_solution.shape[2]
    source_count = sources.shape[3]
    selector = (
        lax.broadcasted_iota(jnp.int32, (source_count, rhs_local), 0) == station_map[None, :]
    ).astype(jnp.float32)
    adjoint_rhs = jnp.einsum("kcps,sr->kcpr", sources, selector, precision=lax.Precision.HIGHEST)
    partial_value = conj_tproduct(
        lax.all_gather(tail_factor, "col", axis=2, tiled=True), tail_solution
    )
    partial_value = partial_value.reshape(2, panel_count, panel_width, rhs_local)
    solved = [None] * panel_count
    rounded = [None] * panel_count
    row_offset = lax.axis_index("row") * local_rows
    own_rhs = jnp.transpose(adjoint_rhs, (1, 0, 2, 3))
    placed_all = lax.dynamic_update_slice_in_dim(
        jnp.zeros_like(partial_value), own_rhs, row_offset, 2
    )
    base_rhs = lax.psum(placed_all - partial_value, "row")
    whole_coupling = lax.all_gather(coupling, "row", axis=2, tiled=True)
    gathered = [None] * panel_count
    for panel_index in range(panel_count - 1, -1, -1):
        full_y = base_rhs[:, panel_index]
        for later_panel in range(panel_index + 1, panel_count):
            block_cols = whole_coupling[later_panel][
                :, :, panel_index * panel_width : (panel_index + 1) * panel_width
            ]
            full_y = full_y - conj_tproduct(block_cols, gathered[later_panel])
        solved[panel_index] = complex_product(inverse_blocks[panel_index], full_y)
        rounded[panel_index] = solved[panel_index].astype(jnp.bfloat16)
        if panel_index > 0:
            gathered[panel_index] = lax.all_gather(rounded[panel_index], "row", axis=1, tiled=True)
    return jnp.stack(solved)


def split_two(value):
    high = value.astype(jnp.bfloat16)
    low = (value - high.astype(jnp.float32)).astype(jnp.bfloat16)
    return high, low


def dot_tn(left, right):
    return lax.dot_general(
        left, right, (((0,), (0,)), ((), ())), preferred_element_type=jnp.float32
    )


def dot_nt(left, right):
    return lax.dot_general(
        left, right, (((1,), (1,)), ((), ())), preferred_element_type=jnp.float32
    )


def dot_nn(left, right):
    return lax.dot_general(
        left, right, (((1,), (0,)), ((), ())), preferred_element_type=jnp.float32
    )


def panel_pairs(panels):
    return [(j, k) for j in range(panels) for k in range(j)]


def fused_kernel(
    rows, depth, panels, chunks,
    factor_h, tail_h, coupling_h, inverse_h, sources_h, station_h, out,
    factor, tail, coupling, inverse, sources, station, rx, part, core_in, core_sum, y_in, y_sum, z_in, reduced, far_in,
    core_low, y_low, z_low, sol_in,
    blocks, adj_out, adj_in, sol_out, xs, adj_s, sol_s, core_s, y_s, z_s, far_s,
    bz_s, by_s, bc_s, load_s,
):
    row = lax.axis_index("row")
    col = lax.axis_index("col")
    core = lax.rem(row, 2)
    yy = lax.rem(row // 2, 2)
    zz = row // 4
    width = factor.shape[2]
    local = inverse.shape[2]
    panel = inverse.shape[3]
    span = rows * 8
    lanes = adj_in.shape[3]
    kinds = panels * 2

    def slot_of(r):
        return (lax.rem(r, 2) * 2 + lax.rem(r // 2, 2)) * depth + r // 4

    def row_of(z, y, c):
        return z * 4 + y * 2 + c

    my_slot = slot_of(row)
    peers = [lax.rem(row + d, rows) for d in range(1, rows)]
    core_peer = row_of(zz, yy, 1 - core)
    y_peer = row_of(zz, 1 - yy, core)
    z_hops = [lax.rem(zz + d, depth) for d in range(1, depth)]
    z_from = [lax.rem(zz + depth - d, depth) for d in range(1, depth)]
    pending = []

    def send(source, target, sems, device_row, device_col, *index):
        copy = pltpu.make_async_remote_copy(
            src_ref=source, dst_ref=target,
            send_sem=sems.at[(0, *index)], recv_sem=sems.at[(1, *index)],
            device_id=(device_row, device_col), device_id_type=MESH,
        )
        copy.start()
        pending.append(copy)
        return copy

    loads = []
    for n, (source, target) in enumerate((
        (inverse_h, inverse), (coupling_h, coupling), (tail_h, tail),
        (factor_h, factor), (sources_h, sources), (station_h, station),
    )):
        load = pltpu.make_async_copy(source, target, load_s.at[n])
        load.start()
        loads.append(load)
    barrier = pltpu.get_barrier_semaphore()
    for peer in peers:
        pl.semaphore_signal(barrier, inc=1, device_id=(peer, col), device_id_type=MESH)
    for z in [zz] + z_hops:
        pl.semaphore_signal(
            barrier, inc=1, device_id=(row_of(z, yy, core), 1 - col), device_id_type=MESH
        )

    loads[0].wait()
    loads[1].wait()
    pairs = panel_pairs(panels)
    for k in range(panels):
        for c in range(2):
            high, low = split_two(inverse[k, c])
            blocks[row, k * 2 + c] = high
            blocks[row, kinds + k * 2 + c] = low
    for place, (j, k) in enumerate(pairs):
        for c in range(2):
            blocks[row, 2 * kinds + place * 2 + c] = coupling[
                j, c, :, k * panel:(k + 1) * panel
            ]
    pl.semaphore_wait(barrier, rows - 1 + depth)

    def send_x(q):
        return send(tail_h.at[:, :, pl.ds(q * span, span)], rx.at[q], xs, row, 1 - col, q)

    x_copies = [send_x(0)]

    bz = [
        send(blocks.at[row], blocks.at[row], bz_s, row_of(z, yy, core), col, d)
        for d, z in enumerate(z_hops)
    ]
    by = [send(blocks.at[row], blocks.at[row], by_s, y_peer, col, 0)]
    bc = [send(blocks.at[row], blocks.at[row], bc_s, core_peer, col, 0)]

    def multiply(real, imag):
        re = dot_tn(real, factor[0]) + dot_tn(imag, factor[1])
        im = dot_tn(imag, factor[0]) - dot_tn(real, factor[1])
        return re, im

    core_copies, y_copies, z_copies = {}, {}, {}

    def stage_core(chunk, real, imag):
        re, im = multiply(real, imag)
        shape = (2, 2, depth, 8, width)
        part[chunk, :, :, :, 0:8, :] = re.reshape(shape)
        part[chunk, :, :, :, 8:16, :] = im.reshape(shape)
        core_copies[chunk] = send(
            part.at[chunk, 1 - core], core_in.at[chunk], core_s, core_peer, col, chunk
        )

    def stage_y(chunk):
        core_copies[chunk].wait_recv()
        core_sum[chunk] = part[chunk, core] + core_in[chunk]
        if chunk >= chunks:
            late = chunk - chunks
            core_low[late] = core_sum[chunk, 1 - yy].astype(jnp.bfloat16)
            y_copies[chunk] = send(core_low.at[late], y_low.at[late], y_s, y_peer, col, chunk)
            return
        y_copies[chunk] = send(
            core_sum.at[chunk, 1 - yy], y_in.at[chunk], y_s, y_peer, col, chunk
        )

    def stage_z(chunk):
        y_copies[chunk].wait_recv()
        if chunk >= chunks:
            late = chunk - chunks
            z_low[late] = (core_sum[chunk, yy] + y_low[late].astype(jnp.float32)).astype(jnp.bfloat16)
            z_copies[chunk] = [
                send(
                    z_low.at[late, z], far_in.at[late, d], far_s,
                    row_of(z, yy, core), 1 - col, late, d,
                )
                for d, z in enumerate([zz] + z_hops)
            ]
            return
        y_sum[chunk] = core_sum[chunk, yy] + y_in[chunk]
        z_copies[chunk] = [
            send(y_sum.at[chunk, z], z_in.at[chunk, d], z_s, row_of(z, yy, core), col, chunk, d)
            for d, z in enumerate(z_hops)
        ]

    def stage_end(chunk):
        total = y_sum[chunk, zz]
        for d, copy in enumerate(z_copies[chunk]):
            copy.wait_recv()
            total = total + z_in[chunk, d]
        reduced[chunk] = total

    loads[2].wait()
    loads[3].wait()
    for q in range(chunks):
        stage_core(q, tail[0, :, q * span:(q + 1) * span], tail[1, :, q * span:(q + 1) * span])

    loads[4].wait()
    loads[5].wait()
    count = sources.shape[3]
    selector = (
        lax.broadcasted_iota(jnp.int32, (count, tail.shape[2]), 0) == station[...]
    ).astype(jnp.float32).astype(jnp.bfloat16)
    flat = sources[...].reshape(kinds * local, count)
    if lanes > kinds * local:
        flat = jnp.concatenate(
            [flat, jnp.zeros((lanes - kinds * local, count), jnp.float32)], axis=0
        )
    first, rest = split_two(flat)
    rest = flat - first.astype(jnp.float32)
    second, third = split_two(rest)
    taken = dot_tn(selector, jnp.transpose(first)) + dot_tn(selector, jnp.transpose(second))
    taken = taken + dot_tn(selector, jnp.transpose(third))
    for q in range(chunks):
        adj_out[:, q] = taken[q * span:(q + 1) * span].reshape(rows, 8, lanes)
    adj_copies = [
        send(adj_out.at[slot_of(peer)], adj_in.at[row], adj_s, peer, col, d)
        for d, peer in enumerate(peers)
    ]
    adj_in[row] = adj_out[my_slot]

    x_copies += [send_x(q) for q in range(1, chunks)]
    for q in range(chunks):
        stage_y(q)
    for d in range(depth - 1):
        bz[d].wait_recv()
        place = blocks.at[row_of(z_from[d], yy, core)]
        by.append(send(place, place, by_s, y_peer, col, d + 1))
        bc.append(send(place, place, bc_s, core_peer, col, d + 1))
    for q in range(chunks):
        stage_z(q)

    for q in range(chunks):
        x_copies[q].wait_recv()
        stage_core(chunks + q, rx[q, 0], rx[q, 1])
        if q == 0:
            for own_chunk in range(chunks):
                stage_end(own_chunk)
        stage_y(chunks + q)
        stage_z(chunks + q)
        if q == 0:
            for copy in adj_copies:
                copy.wait_recv()
            received = [adj_in[r].reshape(chunks * 8, lanes) for r in range(rows)]
            adjoint = [
                jnp.concatenate(
                    [piece[:, n * local:(n + 1) * local] for piece in received], axis=1
                )
                for n in range(kinds)
            ]
            for d, z in enumerate([zz] + z_from):
                by[d].wait_recv()
                place = blocks.at[row_of(z, 1 - yy, core)]
                bc.append(send(place, place, bc_s, core_peer, col, depth + d))
    for copy in bc:
        copy.wait_recv()
    others = []
    for q in range(chunks):
        total = None
        for d, copy in enumerate(z_copies[chunks + q]):
            copy.wait_recv()
            piece = far_in[q, d].astype(jnp.float32)
            total = piece if total is None else total + piece
        others.append(total)

    owns = [reduced[q] for q in range(chunks)]
    sums = []
    for c in range(2):
        own = jnp.concatenate([value[c * 8:(c + 1) * 8] for value in owns], axis=0)
        other = jnp.concatenate([value[c * 8:(c + 1) * 8] for value in others], axis=0)
        lower = jnp.where(col == 0, own, other)
        upper = jnp.where(col == 0, other, own)
        sums.append(jnp.concatenate([lower, upper], axis=1))

    def block(n):
        return blocks[:, n].reshape(panel, panel)

    count_r = chunks * 8
    rounded = [None] * panels
    solved = [None] * kinds
    for k in range(panels - 1, -1, -1):
        real = sums[0][:, k * panel:(k + 1) * panel]
        imag = sums[1][:, k * panel:(k + 1) * panel]
        for j in range(k + 1, panels):
            place = 2 * kinds + pairs.index((j, k)) * 2
            with_real = dot_nn(rounded[j], block(place))
            with_imag = dot_nn(rounded[j], block(place + 1))
            real = real + with_real[:count_r] + with_imag[count_r:]
            imag = imag + with_real[count_r:] - with_imag[:count_r]
        residue = jnp.concatenate([adjoint[k * 2] - real, adjoint[k * 2 + 1] - imag], axis=0)
        high, low = split_two(residue)
        both = jnp.concatenate([high, low], axis=0)
        products = []
        for c in range(2):
            wide = dot_nt(both, block(k * 2 + c))
            fine = dot_nt(high, block(kinds + k * 2 + c))
            products.append(wide[:2 * count_r] + wide[2 * count_r:] + fine)
        solved[k * 2] = products[0][:count_r] - products[1][count_r:]
        solved[k * 2 + 1] = products[0][count_r:] + products[1][:count_r]
        rounded[k] = jnp.concatenate([solved[k * 2], solved[k * 2 + 1]], axis=0).astype(jnp.bfloat16)
    filler = [jnp.zeros((count_r, lanes - kinds * local), jnp.float32)] if lanes > kinds * local else []
    for r in range(rows):
        pieces = [value[:, r * local:(r + 1) * local] for value in solved] + filler
        sol_out[r] = jnp.concatenate(pieces, axis=1)
    sol_copies = [
        send(sol_out.at[peer], sol_in.at[my_slot], sol_s, peer, col, d)
        for d, peer in enumerate(peers)
    ]
    sol_in[my_slot] = sol_out[row]
    for copy in sol_copies:
        copy.wait_recv()
    found = sol_in[...]
    for q in range(chunks):
        turned = jnp.transpose(found[:, q * 8:(q + 1) * 8].reshape(span, lanes))
        out[:, :, :, q * span:(q + 1) * span] = turned[:kinds * local].reshape(
            panels, 2, local, span
        )
    for copy in pending:
        copy.wait_send()


def fused_shards(rows, tail_factor, tail_solution, coupling, inverse_blocks, sources, station_map):
    panels, _, local, panel = inverse_blocks.shape
    depth = rows // 4
    width = tail_factor.shape[2]
    rhs = tail_solution.shape[2]
    tall = tail_solution.shape[1]
    chunks = rhs // (rows * 8)
    lanes = -(-panels * 2 * local // 128) * 128
    kept = 4 * panels + panels * (panels - 1)
    vmem = pl.BlockSpec(memory_space=pltpu.VMEM)
    f32, bf16 = jnp.float32, jnp.bfloat16
    sem = pltpu.SemaphoreType.DMA
    return pl.pallas_call(
        functools.partial(fused_kernel, rows, depth, panels, chunks),
        out_shape=jax.ShapeDtypeStruct((panels, 2, local, rhs), f32),
        in_specs=[pl.BlockSpec(memory_space=pltpu.HBM)] * 6,
        out_specs=vmem,
        scratch_shapes=[
            pltpu.VMEM(tail_factor.shape, bf16),
            pltpu.VMEM(tail_solution.shape, bf16),
            pltpu.VMEM(coupling.shape, bf16),
            pltpu.VMEM(inverse_blocks.shape, f32),
            pltpu.VMEM(sources.shape, f32),
            pltpu.VMEM((1, rhs), jnp.int32),
            pltpu.VMEM((chunks, 2, tall, rows * 8), bf16),
            pltpu.VMEM((2 * chunks, 2, 2, depth, 16, width), f32),
            pltpu.VMEM((2 * chunks, 2, depth, 16, width), f32),
            pltpu.VMEM((2 * chunks, 2, depth, 16, width), f32),
            pltpu.VMEM((chunks, depth, 16, width), f32),
            pltpu.VMEM((chunks, depth, 16, width), f32),
            pltpu.VMEM((chunks, depth - 1, 16, width), f32),
            pltpu.VMEM((chunks, 16, width), f32),
            pltpu.VMEM((chunks, depth, 16, width), bf16),
            pltpu.VMEM((chunks, depth, 16, width), bf16),
            pltpu.VMEM((chunks, depth, 16, width), bf16),
            pltpu.VMEM((chunks, depth, 16, width), bf16),
            pltpu.VMEM((rows, chunks * 8, lanes), f32),
            pltpu.VMEM((rows, kept, local, panel), bf16),
            pltpu.VMEM((rows, chunks, 8, lanes), f32),
            pltpu.VMEM((rows, chunks, 8, lanes), f32),
            pltpu.VMEM((rows, chunks * 8, lanes), f32),
            sem((2, chunks)),
            sem((2, rows - 1)),
            sem((2, rows - 1)),
            sem((2, 2 * chunks)),
            sem((2, 2 * chunks)),
            sem((2, chunks, depth - 1)),
            sem((2, chunks, depth)),
            sem((2, depth - 1)),
            sem((2, depth)),
            sem((2, 2 * depth)),
            sem((6,)),
        ],
        compiler_params=pltpu.CompilerParams(
            collective_id=0, has_side_effects=True, vmem_limit_bytes=63 * 1024 * 1024
        ),
    )(tail_factor, tail_solution, coupling, inverse_blocks, sources, station_map[None, :])


def plan(mesh):
    rows, cols = mesh.shape["row"], mesh.shape["col"]

    def body(tail_factor, tail_solution, coupling, inverse_blocks, sources, station_map):
        fits = (
            cols == 2
            and rows % 4 == 0
            and rows >= 8
            and tail_factor.shape[2] % 128 == 0
            and (rows * 8) % 128 == 0
            and tail_solution.shape[2] % (rows * 16) == 0
            and inverse_blocks.shape[2] % 16 == 0
            and inverse_blocks.shape[3] % 128 == 0
        )
        arrays = (tail_factor, tail_solution, coupling, inverse_blocks, sources, station_map)
        return fused_shards(rows, *arrays) if fits else shards(*arrays)

    return body


def solution(mesh):
    placed = (
        P(None, "row", "col"),
        P(None, "row", "col"),
        P(None, None, "row", None),
        P(None, None, "row", None),
        P(None, None, "row", None),
        P("col"),
    )
    return jax.shard_map(
        plan(mesh), mesh=mesh, in_specs=placed, out_specs=P(None, None, "row", "col"), check_vma=False
    )
```
